32 devices in a mesh: rows: 2 (over x), chan: 16 (over z, y, core).
Axes of the slice: x: 2, y: 2, z: 4, core: 2. Of those that a mesh axis runs over, the one named last changes fastest.
Arguments:
- pair_rep: bfloat16 [512, 512, 128], P('rows', 'chan'), may hold values from -6 to 6
- upstream: bfloat16 [512, 512, 128], P('rows', 'chan'), may hold values from -8 to 8
- out_proj: bfloat16 [128, 512], replicated, may hold values from -0.5 to 0.5
- out_gate: bfloat16 [128, 128], replicated, may hold values from -0.5 to 0.5
- out_final: bfloat16 [128, 128], replicated, may hold values from -0.5 to 0.5
- in_proj: bfloat16 [128, 512], replicated, may hold values from -0.5 to 0.5
- in_gate: bfloat16 [128, 128], replicated, may hold values from -0.5 to 0.5
- in_final: bfloat16 [128, 128], replicated, may hold values from -0.5 to 0.5
- out_drop: int32 [512, 128], P('chan'), may hold values 0 or 1
- in_drop: int32 [512, 128], P('chan'), may hold values 0 or 1
Outputs:
- final_pair: bfloat16 [512, 512, 128], P('rows', 'chan')
- grad_pair: bfloat16 [512, 512, 128], P('rows', 'chan')
- grad_proj: float32 [128, 512], replicated
- grad_gate: float32 [128, 128], replicated
- grad_final: float32 [128, 128], replicated
The draws below stay inside these ranges and needn't reach their ends.
All inputs are finite; a program needn't handle non-finite values. No bound on the sum of `out_drop` or of `in_drop` on one device may be relied on, other than what follows from the above.
Results may differ from the reference program's by a relative error of at most 0.0097.
Values may be sent and summed in bfloat16 or wider, within the bound.
A program may use at most 192 MiB of HBM per device.

```python
import math
import jax
import jax.numpy as jnp
from jax import lax

C = 128
H = 128
N = 512


def draw_upstream(key, part):
    key = jax.random.fold_in(key, 7)
    row_key, col_key, body_key = jax.random.split(key, 3)
    row_scale = jnp.exp(jax.random.uniform(row_key, (N, 1, 1), jnp.float32, 0.0, math.log(10.0)))
    col_scale = jnp.exp(jax.random.uniform(col_key, (1, N, 1), jnp.float32, 0.0, math.log(10.0)))
    gaussian = jax.random.normal(body_key, (N, N, C), jnp.float32)
    return jnp.clip(gaussian * row_scale * col_scale * 0.1, -8.0, 8.0).astype(jnp.bfloat16)


def plant(drawn, rng, low, high):
    dims = drawn.shape
    index_at = [jax.random.randint(jax.random.fold_in(rng, axis), (), 0, dims[axis]) for axis in range(len(dims))]
    drawn = drawn.at[tuple(index_at)].set(low)
    longest = dims.index(max(dims))
    index_at[longest] = (index_at[longest] + 1) % dims[longest]
    return drawn.at[tuple(index_at)].set(high)


def level_of(rng, dims, shards, smallest, largest):
    gain = 1.0
    for position, blocks in shards:
        steps = jax.random.uniform(jax.random.fold_in(jax.random.fold_in(rng, 6), position), (blocks,), jnp.float32, smallest / len(shards), largest / len(shards))
        gain = gain * jnp.repeat(jnp.exp(steps), dims[position] // blocks).reshape((-1,) + (1,) * (len(dims) - 1 - position))
    return gain


def bell_draw(stream_key, dims, width, reach, cuts=(), held_as=jnp.bfloat16):
    drawn = jax.random.normal(stream_key, dims, jnp.float32) * width
    if len(cuts) > 0:
        drawn = level_of(stream_key, dims, cuts, -0.22, 0.18) * drawn
    return jnp.clip(drawn, min=-reach, max=reach).astype(held_as)


def setup_inputs(seed: int = 0) -> dict:
    key_of = jax.random.split(jax.random.key(seed), 11)
    pair_rep = bell_draw(key_of[0], (N, N, C), 1.0, 6.0, ((0, 2), (1, 16)))
    upstream = draw_upstream(jax.random.fold_in(key_of[10], 71), 0)
    out_proj = bell_draw(key_of[2], (C, 4 * H), C ** -0.5, 0.5)
    out_gate = bell_draw(key_of[3], (C, C), C ** -0.5, 0.5)
    out_final = bell_draw(key_of[4], (H, C), H ** -0.5, 0.5)
    in_proj = bell_draw(key_of[5], (C, 4 * H), C ** -0.5, 0.5)
    in_gate = bell_draw(key_of[6], (C, C), C ** -0.5, 0.5)
    in_final = bell_draw(key_of[7], (H, C), H ** -0.5, 0.5)
    out_drop = plant((jax.random.randint(key_of[8], (N, C), 0, 4) < 3).astype(jnp.int32), jax.random.fold_in(key_of[8], 1), 0, 1)
    in_drop = plant((jax.random.randint(key_of[9], (N, C), 0, 4) < 3).astype(jnp.int32), jax.random.fold_in(key_of[9], 1), 0, 1)
    return dict(pair_rep=pair_rep, upstream=upstream, out_proj=out_proj, out_gate=out_gate, out_final=out_final, in_proj=in_proj, in_gate=in_gate, in_final=in_final, out_drop=out_drop, in_drop=in_drop)


epsilon = 1e-05
keep_rate = 0.75

def widen(values):
    return values.astype(jnp.float32)

def layer_norm(values, along):
    average = lax.optimization_barrier(jnp.mean(values, axis=along, keepdims=True))
    centred = values - average
    inv_std = lax.rsqrt(lax.optimization_barrier(jnp.mean(centred * centred, axis=along, keepdims=True)) + epsilon)
    return (centred * inv_std, inv_std)

def norm_back(gradient, scaled, inv_std, along):
    first_mean = lax.optimization_barrier(jnp.mean(gradient, axis=along, keepdims=True))
    second_mean = lax.optimization_barrier(jnp.mean(gradient * scaled, axis=along, keepdims=True))
    return inv_std * (gradient - first_mean - scaled * second_mean)

def front(pair_in, proj_w, gate_w):
    scaled, inv_std = layer_norm(pair_in.astype(jnp.float32), 2)
    normed = scaled.astype(jnp.bfloat16).reshape(-1, C)
    projected = jnp.dot(widen(normed), widen(proj_w)).T
    gate_act = jax.nn.sigmoid(jnp.dot(widen(normed), widen(gate_w)))
    left_proj = (jax.nn.sigmoid(projected[:H]) * projected[H:2 * H]).astype(jnp.bfloat16).reshape(H, N, N)
    right_proj = (jax.nn.sigmoid(projected[2 * H:3 * H]) * projected[3 * H:]).astype(jnp.bfloat16).reshape(H, N, N)
    return (scaled, inv_std, normed, projected, gate_act, left_proj, right_proj)

def finish(triangle, gate_act, final_w, pair_in, drop_mask):
    tri_hat, tri_inv = layer_norm(triangle.reshape(H, -1).astype(jnp.float32), 0)
    tri_normed = tri_hat.astype(jnp.bfloat16)
    out_rows = jnp.dot(widen(tri_normed).T, widen(final_w))
    update = gate_act * out_rows
    new_pair = (pair_in.astype(jnp.float32) + drop_mask.astype(jnp.float32)[None] * update.reshape(pair_in.shape) / keep_rate).astype(jnp.bfloat16)
    return (tri_hat, tri_inv, tri_normed, out_rows, new_pair)

def reference(pair_rep, upstream, out_proj, out_gate, out_final, in_proj, in_gate, in_final, out_drop, in_drop):
    scaled, inv_std, normed, projected, gate_act, left_proj, right_proj = front(pair_rep, out_proj, out_gate)
    triangle = jnp.einsum('hik,hjk->hij', widen(left_proj), widen(right_proj)).astype(jnp.bfloat16)
    tri_hat, tri_inv, tri_normed, out_rows, middle = finish(triangle, gate_act, out_final, pair_rep, out_drop)
    update_grad = (upstream.astype(jnp.float32) * out_drop.astype(jnp.float32)[None] / keep_rate).reshape(-1, C)
    gate_grad = update_grad * out_rows
    out_grad = (update_grad * gate_act).astype(jnp.bfloat16)
    normed_grad = jnp.dot(widen(out_final), widen(out_grad).T)
    tri_grad = norm_back(normed_grad, tri_hat, tri_inv, 0).astype(jnp.bfloat16).reshape(H, N, N)
    pre_grad = (gate_grad * gate_act * (1.0 - gate_act)).astype(jnp.bfloat16)
    tri_float = widen(tri_grad)
    left_grad = jnp.einsum('hij,hjk->hik', tri_float, widen(right_proj)).astype(jnp.bfloat16)
    right_grad = jnp.einsum('hij,hik->hjk', tri_float, widen(left_proj)).astype(jnp.bfloat16)
    left_back = left_grad.reshape(H, -1).astype(jnp.float32)
    right_back = right_grad.reshape(H, -1).astype(jnp.float32)
    left_sig = jax.nn.sigmoid(projected[:H])
    right_sig = jax.nn.sigmoid(projected[2 * H:3 * H])
    proj_grad = jnp.concatenate([left_back * projected[H:2 * H] * left_sig * (1.0 - left_sig), left_back * left_sig, right_back * projected[3 * H:] * right_sig * (1.0 - right_sig), right_back * right_sig], 0).astype(jnp.bfloat16)
    input_grad = jnp.dot(widen(proj_grad).T, widen(out_proj).T)
    input_grad = input_grad + jnp.dot(widen(pre_grad), widen(out_gate).T)
    grad_pair = (upstream.astype(jnp.float32) + norm_back(input_grad.reshape(N, N, C), scaled, inv_std, 2)).astype(jnp.bfloat16)
    grad_proj = jnp.dot(widen(normed).T, widen(proj_grad).T) / N
    grad_gate = jnp.dot(widen(normed).T, widen(pre_grad)) / N
    grad_final = jnp.dot(widen(tri_normed), widen(out_grad)) / N
    two_parts = front(middle, in_proj, in_gate)
    gate_two, left_two, right_two = (two_parts[4], two_parts[5], two_parts[6])
    tri_two = jnp.einsum('hki,hkj->hij', widen(left_two), widen(right_two)).astype(jnp.bfloat16)
    final_pair = finish(tri_two, gate_two, in_final, middle, in_drop)[4]
    return (final_pair, grad_pair, grad_proj, grad_gate, grad_final)
```

```python
import functools

import jax
import jax.numpy as jnp
from jax import lax
from jax.experimental import pallas as pl
from jax.experimental.pallas import tpu as pltpu
from jax.sharding import PartitionSpec as P

N = 512
H = 128

epsilon = 1e-05
keep_rate = 0.75

BOTH = ("rows", "chan")
STEP = 4
GRANT = 40 * 1024 * 1024
F32 = jnp.float32
BF16 = jnp.bfloat16
NN = (((1,), (0,)), ((), ()))
NT = (((1,), (1,)), ((), ()))
TN = (((0,), (0,)), ((), ()))


def mm(a, b, dims=NN):
    return lax.dot_general(a, b, dims, preferred_element_type=F32)


def norm_cols(x):
    average = jnp.mean(x, axis=0, keepdims=True)
    centred = x - average
    inv_std = lax.rsqrt(jnp.mean(centred * centred, axis=0, keepdims=True) + epsilon)
    return centred * inv_std, inv_std


def sides(normed, proj_t, left_ref, right_ref, at):
    hidden = proj_t.shape[0] // 4
    projected = mm(proj_t, normed)
    a_gate, a_val = projected[:hidden], projected[hidden : 2 * hidden]
    b_gate, b_val = projected[2 * hidden : 3 * hidden], projected[3 * hidden :]
    left_ref[at] = (jax.nn.sigmoid(a_gate) * a_val).astype(BF16)
    right_ref[at] = (jax.nn.sigmoid(b_gate) * b_val).astype(BF16)


def front_kernel(pair_ref, proj_ref, left_ref, right_ref):
    for at in range(pair_ref.shape[0]):
        scaled, _ = norm_cols(pair_ref[at].astype(F32))
        sides(scaled.astype(BF16), proj_ref[...], left_ref, right_ref, at)


def middle_kernel(
    tri_ref, pair_ref, up_ref, drop_ref, gate_ref, final_t_ref, final_ref, proj_two_ref,
    mid_ref, tri_grad_ref, pre_ref, left_ref, right_ref, grad_gate_ref, grad_final_ref,
):
    @pl.when(pl.program_id(0) == 0)
    def _():
        grad_gate_ref[...] = jnp.zeros_like(grad_gate_ref)
        grad_final_ref[...] = jnp.zeros_like(grad_final_ref)

    for at in range(tri_ref.shape[0]):
        pair = pair_ref[at].astype(F32)
        normed = norm_cols(pair)[0].astype(BF16)
        gate = jax.nn.sigmoid(mm(gate_ref[...], normed))
        tri_hat, tri_inv = norm_cols(tri_ref[at].astype(F32))
        tri_normed = tri_hat.astype(BF16)
        out_rows = mm(final_t_ref[...], tri_normed)
        drop = drop_ref[at]
        middle = (pair + drop * (gate * out_rows)).astype(BF16)
        mid_ref[at] = middle
        update_grad = up_ref[at].astype(F32) * drop
        out_grad = (update_grad * gate).astype(BF16)
        pre_grad = (update_grad * out_rows * gate * (1.0 - gate)).astype(BF16)
        pre_ref[at] = pre_grad
        normed_grad = mm(final_ref[...], out_grad)
        first = jnp.mean(normed_grad, axis=0, keepdims=True)
        second = jnp.mean(normed_grad * tri_hat, axis=0, keepdims=True)
        tri_grad_ref[at] = (tri_inv * (normed_grad - first - tri_hat * second)).astype(BF16)
        grad_gate_ref[...] += mm(normed, pre_grad, NT)
        grad_final_ref[...] += mm(tri_normed, out_grad, NT)
        normed_two = norm_cols(middle.astype(F32))[0].astype(BF16)
        sides(normed_two, proj_two_ref[...], left_ref, right_ref, at)


def back_kernel(
    pair_ref, up_ref, pre_ref, left_ref, right_ref, proj_t_ref, proj_ref, gate_ref,
    grad_ref, grad_proj_ref,
):
    @pl.when(pl.program_id(0) == 0)
    def _():
        grad_proj_ref[...] = jnp.zeros_like(grad_proj_ref)

    hidden = proj_t_ref.shape[0] // 4
    for at in range(pair_ref.shape[0]):
        scaled, inv_std = norm_cols(pair_ref[at].astype(F32))
        normed = scaled.astype(BF16)
        projected = mm(proj_t_ref[...], normed)
        left, right = left_ref[at].astype(F32), right_ref[at].astype(F32)
        left_sig = jax.nn.sigmoid(projected[:hidden])
        right_sig = jax.nn.sigmoid(projected[2 * hidden : 3 * hidden])
        left_val, right_val = left * left_sig, right * right_sig
        proj_grad = jnp.concatenate(
            [
                (left_val * projected[hidden : 2 * hidden] * (1.0 - left_sig)).astype(BF16),
                left_val.astype(BF16),
                (right_val * projected[3 * hidden :] * (1.0 - right_sig)).astype(BF16),
                right_val.astype(BF16),
            ],
            0,
        )
        grad_proj_ref[...] += mm(normed, proj_grad, NT)
        input_grad = mm(proj_ref[...], proj_grad) + mm(gate_ref[...], pre_ref[at])
        first = jnp.mean(input_grad, axis=0, keepdims=True)
        second = jnp.mean(input_grad * scaled, axis=0, keepdims=True)
        grad_ref[at] = (
            up_ref[at].astype(F32) + inv_std * (input_grad - first - scaled * second)
        ).astype(BF16)


def final_kernel(tri_ref, mid_ref, drop_ref, gate_ref, final_t_ref, out_ref):
    for at in range(tri_ref.shape[0]):
        middle = mid_ref[at].astype(F32)
        gate = jax.nn.sigmoid(mm(gate_ref[...], norm_cols(middle)[0].astype(BF16)))
        tri_normed = norm_cols(tri_ref[at].astype(F32))[0].astype(BF16)
        out_rows = mm(final_t_ref[...], tri_normed)
        out_ref[at] = (middle + drop_ref[at] * (gate * out_rows)).astype(BF16)


def pairwise(kernel, by_pair, whole, pair_outs, sum_outs, name):
    steps = by_pair[0].shape[0] // STEP if by_pair[0].shape[0] % STEP == 0 else by_pair[0].shape[0]
    count = by_pair[0].shape[0] // steps
    cut = lambda a: pl.BlockSpec((count,) + a.shape[1:], lambda n: (n, 0, 0))
    full = lambda a: pl.BlockSpec(a.shape, lambda n: (0, 0))
    outs = [jax.ShapeDtypeStruct(by_pair[0].shape, BF16)] * pair_outs
    sums = [jax.ShapeDtypeStruct(s, F32) for s in sum_outs]
    return pl.pallas_call(
        kernel,
        grid=(steps,),
        in_specs=[cut(a) for a in by_pair] + [full(a) for a in whole],
        out_specs=[cut(a) for a in outs] + [full(a) for a in sums],
        out_shape=outs + sums,
        compiler_params=pltpu.CompilerParams(vmem_limit_bytes=GRANT),
        name=name,
    )(*by_pair, *whole)


def outgoing_kernel(left_ref, right_ref, out_ref):
    rows, chan, _, short, long = left_ref.shape
    left = [left_ref[r].reshape(chan * short, long) for r in range(rows)]
    right = [right_ref[r].reshape(chan * short, long) for r in range(rows)]
    part = chan // rows
    for r in range(rows):
        for q in range(rows):
            product = mm(right[q], left[r], TN).astype(BF16)
            out_ref[r, q * part : (q + 1) * part] = product.reshape(part, 1, short, long)


def backward_kernel(grad_ref, left_ref, right_ref, left_grad_ref, right_grad_ref):
    rows, chan, _, short, long = left_ref.shape
    load = lambda ref: [ref[r].reshape(chan * short, long) for r in range(rows)]
    grad, left, right = load(grad_ref), load(left_ref), load(right_ref)
    for r in range(rows):
        total = sum(mm(right[q], grad[r][q * long : (q + 1) * long]) for q in range(rows))
        left_grad_ref[r] = total.astype(BF16).reshape(chan, 1, short, long)
        total = sum(mm(left[q], grad[q][r * long : (r + 1) * long], NT) for q in range(rows))
        right_grad_ref[r] = total.astype(BF16).reshape(chan, 1, short, long)


def incoming_kernel(left_ref, right_ref, out_ref):
    rows, chan, _, short, long = left_ref.shape
    load = lambda ref: [ref[r].reshape(chan * short, long) for r in range(rows)]
    left, right = load(left_ref), load(right_ref)
    for r in range(rows):
        total = sum(mm(right[q], left[q][r * long : (r + 1) * long], NT) for q in range(rows))
        out_ref[r] = total.astype(BF16).reshape(chan, 1, short, long)


def by_channel(kernel, slabs, outs, name):
    rows, chan, per, short, long = slabs[0].shape
    spec = pl.BlockSpec((rows, chan, 1, short, long), lambda n: (0, 0, n, 0, 0))
    return pl.pallas_call(
        kernel,
        grid=(per,),
        in_specs=[spec] * len(slabs),
        out_specs=[spec] * outs,
        out_shape=[jax.ShapeDtypeStruct(slabs[0].shape, BF16)] * outs,
        compiler_params=pltpu.CompilerParams(vmem_limit_bytes=GRANT),
        name=name,
    )(*slabs)


def exchange(values):
    return lax.all_to_all(values, BOTH, split_axis=0, concat_axis=0, tiled=True)


def few_shards(
    rows, chan,
    pair_rep, upstream, out_proj, out_gate, out_final, in_proj, in_gate, in_final, out_drop, in_drop
):
    long, short, channels = pair_rep.shape
    hidden = out_final.shape[0]
    per = hidden // (rows * chan)
    tokens = long * rows

    def to_slab(values):
        sent = exchange(jnp.swapaxes(values, 0, 1))
        return sent.reshape(rows, chan, per, short, long)

    def to_pairs(slab):
        return jnp.swapaxes(exchange(slab.reshape(hidden, short, long)), 0, 1)

    def column(mask):
        return (mask.astype(F32) / keep_rate)[:, :, None]

    pair = jnp.transpose(pair_rep, (1, 2, 0))
    up = jnp.transpose(upstream, (1, 2, 0))
    out_proj_t, in_proj_t = out_proj.T, in_proj.T
    left, right = pairwise(front_kernel, [pair], [out_proj_t], 2, [], "front")
    left, right = to_slab(left), to_slab(right)
    (triangle,) = by_channel(outgoing_kernel, [left, right], 1, "outgoing")
    middle, tri_grad, pre_grad, left_two, right_two, grad_gate, grad_final = pairwise(
        middle_kernel,
        [to_pairs(triangle), pair, up, column(out_drop)],
        [out_gate.T, out_final.T, out_final, in_proj_t],
        5,
        [out_gate.shape, out_final.shape],
        "middle",
    )
    tri_grad = to_slab(tri_grad)
    left_grad, right_grad = by_channel(backward_kernel, [tri_grad, left, right], 2, "backward")
    left_two, right_two = to_slab(left_two), to_slab(right_two)
    (tri_two,) = by_channel(incoming_kernel, [left_two, right_two], 1, "incoming")
    grad_pair, grad_proj = pairwise(
        back_kernel,
        [pair, up, pre_grad, to_pairs(left_grad), to_pairs(right_grad)],
        [out_proj_t, out_proj, out_gate],
        1,
        [out_proj.shape],
        "back",
    )
    grads = jnp.concatenate([grad_proj, grad_gate, grad_final], 1)
    grads = exchange(grads).reshape(rows * chan, -1, grads.shape[1])
    grads = lax.all_gather(jnp.sum(grads, 0) / tokens, BOTH, axis=0, tiled=True)
    (final_pair,) = pairwise(
        final_kernel,
        [to_pairs(tri_two), middle, column(in_drop)],
        [in_gate.T, in_final.T],
        1,
        [],
        "final",
    )
    wide = out_proj.shape[1]
    return (
        jnp.transpose(final_pair, (2, 0, 1)),
        jnp.transpose(grad_pair, (2, 0, 1)),
        grads[:, :wide],
        grads[:, wide : wide + channels],
        grads[:, wide + channels :],
    )


def layer_norm(values, along):
    average = jnp.mean(values, axis=along, keepdims=True)
    centred = values - average
    inv_std = lax.rsqrt(jnp.mean(centred * centred, axis=along, keepdims=True) + epsilon)
    return (centred * inv_std, inv_std)


def norm_back(gradient, scaled, inv_std, along):
    first_mean = jnp.mean(gradient, axis=along, keepdims=True)
    second_mean = jnp.mean(gradient * scaled, axis=along, keepdims=True)
    return inv_std * (gradient - first_mean - scaled * second_mean)


def front(pair_in, proj_w, gate_w):
    row_count, col_count, channels = pair_in.shape
    scaled, inv_std = layer_norm(pair_in.astype(jnp.float32), 2)
    normed = scaled.astype(jnp.bfloat16).reshape(-1, channels)
    projected = lax.dot_general(
        proj_w, normed, (((0,), (1,)), ((), ())), preferred_element_type=jnp.float32
    )
    hidden = projected.shape[0] // 4
    gate_act = jax.nn.sigmoid(jnp.dot(normed, gate_w, preferred_element_type=jnp.float32))
    left_proj = (jax.nn.sigmoid(projected[:hidden]) * projected[hidden : 2 * hidden]).astype(
        jnp.bfloat16
    )
    right_proj = (
        jax.nn.sigmoid(projected[2 * hidden : 3 * hidden]) * projected[3 * hidden :]
    ).astype(jnp.bfloat16)
    left_proj = left_proj.reshape(hidden, row_count, col_count)
    right_proj = right_proj.reshape(hidden, row_count, col_count)
    return (scaled, inv_std, normed, projected, gate_act, left_proj, right_proj)


def finish(triangle, gate_act, final_w, pair_in, drop_mask):
    hidden = triangle.shape[0]
    tri_hat, tri_inv = layer_norm(triangle.reshape(hidden, -1).astype(jnp.float32), 0)
    tri_normed = tri_hat.astype(jnp.bfloat16)
    out_rows = lax.dot_general(
        tri_normed, final_w, (((0,), (0,)), ((), ())), preferred_element_type=jnp.float32
    )
    update = gate_act * out_rows
    new_pair = (
        pair_in.astype(jnp.float32)
        + drop_mask.astype(jnp.float32)[None] * update.reshape(pair_in.shape) / keep_rate
    ).astype(jnp.bfloat16)
    return (tri_hat, tri_inv, tri_normed, out_rows, new_pair)


def shards(
    pair_rep, upstream, out_proj, out_gate, out_final, in_proj, in_gate, in_final, out_drop, in_drop
):
    channels = pair_rep.shape[2]
    scaled, inv_std, normed, projected, gate_act, left_proj, right_proj = front(
        pair_rep, out_proj, out_gate
    )
    hidden = left_proj.shape[0]
    left_slab, right_slab = (
        lax.all_to_all(left_proj, "chan", split_axis=0, concat_axis=2, tiled=True),
        lax.all_to_all(right_proj, "chan", split_axis=0, concat_axis=2, tiled=True),
    )
    triangle = jnp.einsum(
        "hik,hjk->hij",
        left_slab,
        lax.all_gather(right_slab, "rows", axis=1, tiled=True),
        preferred_element_type=jnp.float32,
    )
    tri_pairs = lax.all_to_all(
        triangle.astype(jnp.bfloat16), "chan", split_axis=2, concat_axis=0, tiled=True
    )
    tri_hat, tri_inv, tri_normed, out_rows, middle = finish(
        tri_pairs, gate_act, out_final, pair_rep, out_drop
    )
    update_grad = (
        upstream.astype(jnp.float32) * out_drop.astype(jnp.float32)[None] / keep_rate
    ).reshape(-1, channels)
    gate_grad = update_grad * out_rows
    out_grad = (update_grad * gate_act).astype(jnp.bfloat16)
    normed_grad = lax.dot_general(
        out_final, out_grad, (((1,), (1,)), ((), ())), preferred_element_type=jnp.float32
    )
    tri_grad = (
        norm_back(normed_grad, tri_hat, tri_inv, 0).astype(jnp.bfloat16).reshape(left_proj.shape)
    )
    pre_grad = (gate_grad * gate_act * (1.0 - gate_act)).astype(jnp.bfloat16)
    tri_slab = lax.all_to_all(tri_grad, "chan", split_axis=0, concat_axis=2, tiled=True)
    right_again = lax.all_gather(right_slab, "rows", axis=1, tiled=True)
    left_grad = jnp.einsum(
        "hij,hjk->hik", tri_slab, right_again, preferred_element_type=jnp.float32
    ).astype(jnp.bfloat16)
    left_full = lax.all_gather(left_slab, "rows", axis=1, tiled=True)
    tri_cols = lax.all_to_all(tri_slab, "rows", split_axis=2, concat_axis=1, tiled=True)
    right_grad = jnp.einsum(
        "hij,hik->hjk", tri_cols, left_full, preferred_element_type=jnp.float32
    ).astype(jnp.bfloat16)
    left_pairs, right_pairs = (
        lax.all_to_all(left_grad, "chan", split_axis=2, concat_axis=0, tiled=True),
        lax.all_to_all(right_grad, "chan", split_axis=2, concat_axis=0, tiled=True),
    )
    left_back = left_pairs.reshape(hidden, -1).astype(jnp.float32)
    right_back = right_pairs.reshape(hidden, -1).astype(jnp.float32)
    left_sig = jax.nn.sigmoid(projected[:hidden])
    right_sig = jax.nn.sigmoid(projected[2 * hidden : 3 * hidden])
    proj_grad = jnp.concatenate(
        [
            left_back * projected[hidden : 2 * hidden] * left_sig * (1.0 - left_sig),
            left_back * left_sig,
            right_back * projected[3 * hidden :] * right_sig * (1.0 - right_sig),
            right_back * right_sig,
        ],
        0,
    ).astype(jnp.bfloat16)
    input_grad = lax.dot_general(
        proj_grad, out_proj, (((0,), (1,)), ((), ())), preferred_element_type=jnp.float32
    )
    input_grad = input_grad + lax.dot_general(
        pre_grad, out_gate, (((1,), (1,)), ((), ())), preferred_element_type=jnp.float32
    )
    grad_pair = (
        upstream.astype(jnp.float32)
        + norm_back(input_grad.reshape(pair_rep.shape), scaled, inv_std, 2)
    ).astype(jnp.bfloat16)
    grad_proj = lax.dot_general(
        normed, proj_grad, (((0,), (1,)), ((), ())), preferred_element_type=jnp.float32
    )
    grad_gate = lax.dot_general(
        normed, pre_grad, (((0,), (0,)), ((), ())), preferred_element_type=jnp.float32
    )
    grad_final = jnp.dot(tri_normed, out_grad, preferred_element_type=jnp.float32)
    summed = lax.psum((grad_proj, grad_gate, grad_final), ("rows", "chan"))
    two_parts = front(middle, in_proj, in_gate)
    gate_two, left_two, right_two = (two_parts[4], two_parts[5], two_parts[6])
    left_chan, right_chan = (
        lax.all_to_all(left_two, "chan", split_axis=0, concat_axis=2, tiled=True),
        lax.all_to_all(right_two, "chan", split_axis=0, concat_axis=2, tiled=True),
    )
    left_cols = lax.all_to_all(left_chan, "rows", split_axis=2, concat_axis=1, tiled=True)
    tri_two = jnp.einsum(
        "hki,hkj->hij",
        left_cols,
        lax.all_gather(right_chan, "rows", axis=1, tiled=True),
        preferred_element_type=jnp.float32,
    )
    tri_two_pairs = lax.all_to_all(
        tri_two.astype(jnp.bfloat16), "chan", split_axis=2, concat_axis=0, tiled=True
    )
    final_pair = finish(tri_two_pairs, gate_two, in_final, middle, in_drop)[4]
    return (final_pair, grad_pair, summed[0] / N, summed[1] / N, summed[2] / N)


def solution(mesh):
    rows, chan = mesh.shape["rows"], mesh.shape["chan"]
    few = H % (rows * chan) == 0 and chan % rows == 0 and N // rows >= 128 and N // chan >= 16
    shard = functools.partial(few_shards, rows, chan) if few else shards
    in_specs = (
        P("rows", "chan", None),
        P("rows", "chan", None),
        P(),
        P(),
        P(),
        P(),
        P(),
        P(),
        P("chan", None),
        P("chan", None),
    )
    out_specs = (P("rows", "chan", None), P("rows", "chan", None), P(), P(), P())
    return jax.shard_map(shard, mesh=mesh, in_specs=in_specs, out_specs=out_specs, check_vma=False)
```

```python
import functools

import jax
import jax.numpy as jnp
from jax import lax
from jax.experimental import pallas as pl
from jax.experimental.pallas import tpu as pltpu
from jax.sharding import PartitionSpec as P

N = 512
H = 128

epsilon = 1e-05
keep_rate = 0.75

BOTH = ("rows", "chan")
STEP = 4
GRANT = 40 * 1024 * 1024
F32 = jnp.float32
BF16 = jnp.bfloat16
NN = (((1,), (0,)), ((), ()))
NT = (((1,), (1,)), ((), ()))
TN = (((0,), (0,)), ((), ()))


def mm(a, b, dims=NN):
    return lax.dot_general(a, b, dims, preferred_element_type=F32)


def norm_cols(x):
    average = jnp.mean(x, axis=0, keepdims=True)
    centred = x - average
    inv_std = lax.rsqrt(jnp.mean(centred * centred, axis=0, keepdims=True) + epsilon)
    return centred * inv_std, inv_std


def sides(normed, proj_t, left_ref, right_ref, at):
    hidden = proj_t.shape[0] // 4
    projected = mm(proj_t, normed)
    a_gate, a_val = projected[:hidden], projected[hidden : 2 * hidden]
    b_gate, b_val = projected[2 * hidden : 3 * hidden], projected[3 * hidden :]
    left_ref[at] = (jax.nn.sigmoid(a_gate) * a_val).astype(BF16)
    right_ref[at] = (jax.nn.sigmoid(b_gate) * b_val).astype(BF16)


def front_kernel(pair_ref, proj_ref, left_ref, right_ref):
    for at in range(pair_ref.shape[0]):
        scaled, _ = norm_cols(pair_ref[at].astype(F32))
        sides(scaled.astype(BF16), proj_ref[...], left_ref, right_ref, at)


def middle_kernel(
    tri_ref, pair_ref, up_ref, drop_ref, gate_ref, final_t_ref, final_ref, proj_two_ref,
    mid_ref, tri_grad_ref, pre_ref, left_ref, right_ref, grad_gate_ref, grad_final_ref,
):
    @pl.when(pl.program_id(0) == 0)
    def _():
        grad_gate_ref[...] = jnp.zeros_like(grad_gate_ref)
        grad_final_ref[...] = jnp.zeros_like(grad_final_ref)

    for at in range(tri_ref.shape[0]):
        pair = pair_ref[at].astype(F32)
        normed = norm_cols(pair)[0].astype(BF16)
        gate = jax.nn.sigmoid(mm(gate_ref[...], normed))
        tri_hat, tri_inv = norm_cols(tri_ref[at].astype(F32))
        tri_normed = tri_hat.astype(BF16)
        out_rows = mm(final_t_ref[...], tri_normed)
        drop = drop_ref[at]
        middle = (pair + drop * (gate * out_rows)).astype(BF16)
        mid_ref[at] = middle
        update_grad = up_ref[at].astype(F32) * drop
        out_grad = (update_grad * gate).astype(BF16)
        pre_grad = (update_grad * out_rows * gate * (1.0 - gate)).astype(BF16)
        pre_ref[at] = pre_grad
        normed_grad = mm(final_ref[...], out_grad)
        first = jnp.mean(normed_grad, axis=0, keepdims=True)
        second = jnp.mean(normed_grad * tri_hat, axis=0, keepdims=True)
        tri_grad_ref[at] = (tri_inv * (normed_grad - first - tri_hat * second)).astype(BF16)
        grad_gate_ref[...] += mm(normed, pre_grad, NT)
        grad_final_ref[...] += mm(tri_normed, out_grad, NT)
        normed_two = norm_cols(middle.astype(F32))[0].astype(BF16)
        sides(normed_two, proj_two_ref[...], left_ref, right_ref, at)


def back_kernel(
    pair_ref, up_ref, pre_ref, left_ref, right_ref, proj_t_ref, proj_ref, gate_ref,
    grad_ref, grad_proj_ref,
):
    @pl.when(pl.program_id(0) == 0)
    def _():
        grad_proj_ref[...] = jnp.zeros_like(grad_proj_ref)

    hidden = proj_t_ref.shape[0] // 4
    for at in range(pair_ref.shape[0]):
        scaled, inv_std = norm_cols(pair_ref[at].astype(F32))
        normed = scaled.astype(BF16)
        projected = mm(proj_t_ref[...], normed)
        left, right = left_ref[at].astype(F32), right_ref[at].astype(F32)
        left_sig = jax.nn.sigmoid(projected[:hidden])
        right_sig = jax.nn.sigmoid(projected[2 * hidden : 3 * hidden])
        left_val, right_val = left * left_sig, right * right_sig
        proj_grad = jnp.concatenate(
            [
                (left_val * projected[hidden : 2 * hidden] * (1.0 - left_sig)).astype(BF16),
                left_val.astype(BF16),
                (right_val * projected[3 * hidden :] * (1.0 - right_sig)).astype(BF16),
                right_val.astype(BF16),
            ],
            0,
        )
        grad_proj_ref[...] += mm(normed, proj_grad, NT)
        input_grad = mm(proj_ref[...], proj_grad) + mm(gate_ref[...], pre_ref[at])
        first = jnp.mean(input_grad, axis=0, keepdims=True)
        second = jnp.mean(input_grad * scaled, axis=0, keepdims=True)
        grad_ref[at] = (
            up_ref[at].astype(F32) + inv_std * (input_grad - first - scaled * second)
        ).astype(BF16)


def final_kernel(tri_ref, mid_ref, drop_ref, gate_ref, final_t_ref, out_ref):
    for at in range(tri_ref.shape[0]):
        middle = mid_ref[at].astype(F32)
        gate = jax.nn.sigmoid(mm(gate_ref[...], norm_cols(middle)[0].astype(BF16)))
        tri_normed = norm_cols(tri_ref[at].astype(F32))[0].astype(BF16)
        out_rows = mm(final_t_ref[...], tri_normed)
        out_ref[at] = (middle + drop_ref[at] * (gate * out_rows)).astype(BF16)


def pairwise(kernel, by_pair, whole, pair_outs, sum_outs, name):
    steps = by_pair[0].shape[0] // STEP if by_pair[0].shape[0] % STEP == 0 else by_pair[0].shape[0]
    count = by_pair[0].shape[0] // steps
    cut = lambda a: pl.BlockSpec((count,) + a.shape[1:], lambda n: (n, 0, 0))
    full = lambda a: pl.BlockSpec(a.shape, lambda n: (0, 0))
    outs = [jax.ShapeDtypeStruct(by_pair[0].shape, BF16)] * pair_outs
    sums = [jax.ShapeDtypeStruct(s, F32) for s in sum_outs]
    return pl.pallas_call(
        kernel,
        grid=(steps,),
        in_specs=[cut(a) for a in by_pair] + [full(a) for a in whole],
        out_specs=[cut(a) for a in outs] + [full(a) for a in sums],
        out_shape=outs + sums,
        compiler_params=pltpu.CompilerParams(vmem_limit_bytes=GRANT),
        name=name,
    )(*by_pair, *whole)


MESH = pl.DeviceIdType.MESH


def crossed(a, b, size):
    total, bit = 0, 1
    while bit < size:
        total = total + bit * ((a // bit + b // bit) % 2)
        bit *= 2
    return total


def partner(step, rows, chan):
    row = crossed(lax.axis_index("rows"), step // chan, rows)
    col = crossed(lax.axis_index("chan"), step % chan, chan)
    return row, col


def greet(rows, chan):
    barrier = pltpu.get_barrier_semaphore()

    def signal(step, carry):
        pl.semaphore_signal(
            barrier, inc=1, device_id=partner(step, rows, chan), device_id_type=MESH
        )
        return carry

    lax.fori_loop(1, rows * chan, signal, 0)
    pl.semaphore_wait(barrier, rows * chan - 1)


def remote(rows, chan, src, dst, send, recv, at, step):
    row, col = partner(step, rows, chan)
    me = lax.axis_index("rows") * chan + lax.axis_index("chan")
    return pltpu.make_async_remote_copy(
        src.at[row * chan + col],
        dst.at[me],
        send.at[at, step],
        recv.at[at, step],
        device_id=(row, col),
        device_id_type=MESH,
    )


def local(chan, src, dst, send, at):
    me = lax.axis_index("rows") * chan + lax.axis_index("chan")
    return pltpu.make_async_copy(src.at[me], dst.at[me], send.at[at, 0])


def send_all(rows, chan, src, dst, send, recv, at):
    def body(step, carry):
        remote(rows, chan, src, dst, send, recv, at, step).start()
        return carry

    local(chan, src, dst, send, at).start()
    lax.fori_loop(1, rows * chan, body, 0)


def wait_all(rows, chan, src, dst, send, recv, at):
    def body(step, carry):
        remote(rows, chan, src, dst, send, recv, at, step).wait()
        return carry

    local(chan, src, dst, send, at).wait()
    lax.fori_loop(1, rows * chan, body, 0)


def planes(ref, h, rows):
    chan, (_, short, long) = ref.shape[0] // rows, ref.shape[1:]
    return [ref[r * chan : (r + 1) * chan, h].reshape(chan * short, long) for r in range(rows)]


def outgoing_kernel(
    rows, chan, left_in, right_in, left_ref, right_ref, tri_ref, product_ref, send, recv
):
    per, short, long = left_ref.shape[1:]
    part = chan // rows
    moves = [(left_in, left_ref), (right_in, right_ref), (product_ref, tri_ref)]
    greet(rows, chan)
    for at in range(2):
        send_all(rows, chan, *moves[at], send, recv, at)
    for at in range(2):
        wait_all(rows, chan, *moves[at], send, recv, at)

    def body(h, carry):
        left, right = planes(left_ref, h, rows), planes(right_ref, h, rows)
        for r in range(rows):
            for q in range(rows):
                product = mm(right[q], left[r], TN).astype(BF16)
                first = r * chan + q * part
                product_ref[first : first + part, h] = product.reshape(part, short, long)
        return carry

    lax.fori_loop(0, per, body, 0)
    send_all(rows, chan, *moves[2], send, recv, 2)
    wait_all(rows, chan, *moves[2], send, recv, 2)


def backward_kernel(
    rows, chan, grad_in, left_two_in, right_two_in, left_ref, right_ref,
    left_out, right_out, tri_two_ref,
    grad_ref, left_two_ref, right_two_ref, left_grad_ref, right_grad_ref, send, recv,
):
    per, short, long = left_ref.shape[1:]
    moves = [
        (grad_in, grad_ref),
        (left_two_in, left_two_ref),
        (right_two_in, right_two_ref),
        (left_grad_ref, left_out),
        (right_grad_ref, right_out),
    ]
    greet(rows, chan)
    for at in range(3):
        send_all(rows, chan, *moves[at], send, recv, at)
    wait_all(rows, chan, *moves[0], send, recv, 0)

    def back(h, carry):
        grad, left, right = (planes(ref, h, rows) for ref in (grad_ref, left_ref, right_ref))
        for r in range(rows):
            at = slice(r * chan, (r + 1) * chan)
            total = sum(mm(right[q], grad[r][q * long : (q + 1) * long]) for q in range(rows))
            left_grad_ref[at, h] = total.astype(BF16).reshape(chan, short, long)
            total = sum(mm(left[q], grad[q][r * long : (r + 1) * long], NT) for q in range(rows))
            right_grad_ref[at, h] = total.astype(BF16).reshape(chan, short, long)
        return carry

    lax.fori_loop(0, per, back, 0)
    for at in (3, 4):
        send_all(rows, chan, *moves[at], send, recv, at)
    for at in (1, 2):
        wait_all(rows, chan, *moves[at], send, recv, at)

    def two(h, carry):
        left, right = planes(left_two_ref, h, rows), planes(right_two_ref, h, rows)
        for r in range(rows):
            total = sum(mm(right[q], left[q][r * long : (r + 1) * long], NT) for q in range(rows))
            tri_two_ref[r * chan : (r + 1) * chan, h] = total.astype(BF16).reshape(chan, short, long)
        return carry

    lax.fori_loop(0, per, two, 0)
    for at in (3, 4):
        wait_all(rows, chan, *moves[at], send, recv, at)


def fused(kernel, rows, chan, slabs, outs, held, moves, number, name):
    vmem = pl.BlockSpec(memory_space=pltpu.VMEM)
    shape = slabs[0].shape
    return pl.pallas_call(
        functools.partial(kernel, rows, chan),
        in_specs=[vmem] * len(slabs),
        out_specs=[vmem] * outs,
        out_shape=[jax.ShapeDtypeStruct(shape, BF16)] * outs,
        scratch_shapes=[pltpu.VMEM(shape, BF16)] * held
        + [pltpu.SemaphoreType.DMA((moves, rows * chan))] * 2,
        compiler_params=pltpu.CompilerParams(
            collective_id=number, has_side_effects=True, vmem_limit_bytes=GRANT
        ),
        name=name,
    )(*slabs)


def exchange(values):
    return lax.all_to_all(values, BOTH, split_axis=0, concat_axis=0, tiled=True)


def few_shards(
    rows, chan,
    pair_rep, upstream, out_proj, out_gate, out_final, in_proj, in_gate, in_final, out_drop, in_drop
):
    long, short, channels = pair_rep.shape
    hidden = out_final.shape[0]
    per = hidden // (rows * chan)
    tokens = long * rows

    def to_slab(values):
        return jnp.swapaxes(values, 0, 1).reshape(rows * chan, per, short, long)

    def to_pairs(slab):
        return jnp.swapaxes(slab.reshape(hidden, short, long), 0, 1)

    def column(mask):
        return (mask.astype(F32) / keep_rate)[:, :, None]

    pair = jnp.transpose(pair_rep, (1, 2, 0))
    up = jnp.transpose(upstream, (1, 2, 0))
    out_proj_t, in_proj_t = out_proj.T, in_proj.T
    left, right = pairwise(front_kernel, [pair], [out_proj_t], 2, [], "front")
    left, right, triangle = fused(
        outgoing_kernel, rows, chan, [to_slab(left), to_slab(right)], 3, 1, 3, 1, "outgoing"
    )
    middle, tri_grad, pre_grad, left_two, right_two, grad_gate, grad_final = pairwise(
        middle_kernel,
        [to_pairs(triangle), pair, up, column(out_drop)],
        [out_gate.T, out_final.T, out_final, in_proj_t],
        5,
        [out_gate.shape, out_final.shape],
        "middle",
    )
    slabs = [to_slab(tri_grad), to_slab(left_two), to_slab(right_two), left, right]
    left_grad, right_grad, tri_two = fused(
        backward_kernel, rows, chan, slabs, 3, 5, 5, 2, "backward"
    )
    tri_two = exchange(tri_two)
    grad_pair, grad_proj = pairwise(
        back_kernel,
        [pair, up, pre_grad, to_pairs(left_grad), to_pairs(right_grad)],
        [out_proj_t, out_proj, out_gate],
        1,
        [out_proj.shape],
        "back",
    )
    grads = jnp.concatenate([grad_proj, grad_gate, grad_final], 1)
    grads = jnp.sum(exchange(grads).reshape(rows * chan, per, -1), 0) / tokens
    grads = exchange(jnp.broadcast_to(grads[None], (rows * chan,) + grads.shape))
    grads = grads.reshape(hidden, -1)
    (final_pair,) = pairwise(
        final_kernel,
        [to_pairs(tri_two), middle, column(in_drop)],
        [in_gate.T, in_final.T],
        1,
        [],
        "final",
    )
    wide = out_proj.shape[1]
    return (
        jnp.transpose(final_pair, (2, 0, 1)),
        jnp.transpose(grad_pair, (2, 0, 1)),
        grads[:, :wide],
        grads[:, wide : wide + channels],
        grads[:, wide + channels :],
    )


def layer_norm(values, along):
    average = jnp.mean(values, axis=along, keepdims=True)
    centred = values - average
    inv_std = lax.rsqrt(jnp.mean(centred * centred, axis=along, keepdims=True) + epsilon)
    return (centred * inv_std, inv_std)


def norm_back(gradient, scaled, inv_std, along):
    first_mean = jnp.mean(gradient, axis=along, keepdims=True)
    second_mean = jnp.mean(gradient * scaled, axis=along, keepdims=True)
    return inv_std * (gradient - first_mean - scaled * second_mean)


def front(pair_in, proj_w, gate_w):
    row_count, col_count, channels = pair_in.shape
    scaled, inv_std = layer_norm(pair_in.astype(jnp.float32), 2)
    normed = scaled.astype(jnp.bfloat16).reshape(-1, channels)
    projected = lax.dot_general(
        proj_w, normed, (((0,), (1,)), ((), ())), preferred_element_type=jnp.float32
    )
    hidden = projected.shape[0] // 4
    gate_act = jax.nn.sigmoid(jnp.dot(normed, gate_w, preferred_element_type=jnp.float32))
    left_proj = (jax.nn.sigmoid(projected[:hidden]) * projected[hidden : 2 * hidden]).astype(
        jnp.bfloat16
    )
    right_proj = (
        jax.nn.sigmoid(projected[2 * hidden : 3 * hidden]) * projected[3 * hidden :]
    ).astype(jnp.bfloat16)
    left_proj = left_proj.reshape(hidden, row_count, col_count)
    right_proj = right_proj.reshape(hidden, row_count, col_count)
    return (scaled, inv_std, normed, projected, gate_act, left_proj, right_proj)


def finish(triangle, gate_act, final_w, pair_in, drop_mask):
    hidden = triangle.shape[0]
    tri_hat, tri_inv = layer_norm(triangle.reshape(hidden, -1).astype(jnp.float32), 0)
    tri_normed = tri_hat.astype(jnp.bfloat16)
    out_rows = lax.dot_general(
        tri_normed, final_w, (((0,), (0,)), ((), ())), preferred_element_type=jnp.float32
    )
    update = gate_act * out_rows
    new_pair = (
        pair_in.astype(jnp.float32)
        + drop_mask.astype(jnp.float32)[None] * update.reshape(pair_in.shape) / keep_rate
    ).astype(jnp.bfloat16)
    return (tri_hat, tri_inv, tri_normed, out_rows, new_pair)


def shards(
    pair_rep, upstream, out_proj, out_gate, out_final, in_proj, in_gate, in_final, out_drop, in_drop
):
    channels = pair_rep.shape[2]
    scaled, inv_std, normed, projected, gate_act, left_proj, right_proj = front(
        pair_rep, out_proj, out_gate
    )
    hidden = left_proj.shape[0]
    left_slab, right_slab = (
        lax.all_to_all(left_proj, "chan", split_axis=0, concat_axis=2, tiled=True),
        lax.all_to_all(right_proj, "chan", split_axis=0, concat_axis=2, tiled=True),
    )
    triangle = jnp.einsum(
        "hik,hjk->hij",
        left_slab,
        lax.all_gather(right_slab, "rows", axis=1, tiled=True),
        preferred_element_type=jnp.float32,
    )
    tri_pairs = lax.all_to_all(
        triangle.astype(jnp.bfloat16), "chan", split_axis=2, concat_axis=0, tiled=True
    )
    tri_hat, tri_inv, tri_normed, out_rows, middle = finish(
        tri_pairs, gate_act, out_final, pair_rep, out_drop
    )
    update_grad = (
        upstream.astype(jnp.float32) * out_drop.astype(jnp.float32)[None] / keep_rate
    ).reshape(-1, channels)
    gate_grad = update_grad * out_rows
    out_grad = (update_grad * gate_act).astype(jnp.bfloat16)
    normed_grad = lax.dot_general(
        out_final, out_grad, (((1,), (1,)), ((), ())), preferred_element_type=jnp.float32
    )
    tri_grad = (
        norm_back(normed_grad, tri_hat, tri_inv, 0).astype(jnp.bfloat16).reshape(left_proj.shape)
    )
    pre_grad = (gate_grad * gate_act * (1.0 - gate_act)).astype(jnp.bfloat16)
    tri_slab = lax.all_to_all(tri_grad, "chan", split_axis=0, concat_axis=2, tiled=True)
    right_again = lax.all_gather(right_slab, "rows", axis=1, tiled=True)
    left_grad = jnp.einsum(
        "hij,hjk->hik", tri_slab, right_again, preferred_element_type=jnp.float32
    ).astype(jnp.bfloat16)
    left_full = lax.all_gather(left_slab, "rows", axis=1, tiled=True)
    tri_cols = lax.all_to_all(tri_slab, "rows", split_axis=2, concat_axis=1, tiled=True)
    right_grad = jnp.einsum(
        "hij,hik->hjk", tri_cols, left_full, preferred_element_type=jnp.float32
    ).astype(jnp.bfloat16)
    left_pairs, right_pairs = (
        lax.all_to_all(left_grad, "chan", split_axis=2, concat_axis=0, tiled=True),
        lax.all_to_all(right_grad, "chan", split_axis=2, concat_axis=0, tiled=True),
    )
    left_back = left_pairs.reshape(hidden, -1).astype(jnp.float32)
    right_back = right_pairs.reshape(hidden, -1).astype(jnp.float32)
    left_sig = jax.nn.sigmoid(projected[:hidden])
    right_sig = jax.nn.sigmoid(projected[2 * hidden : 3 * hidden])
    proj_grad = jnp.concatenate(
        [
            left_back * projected[hidden : 2 * hidden] * left_sig * (1.0 - left_sig),
            left_back * left_sig,
            right_back * projected[3 * hidden :] * right_sig * (1.0 - right_sig),
            right_back * right_sig,
        ],
        0,
    ).astype(jnp.bfloat16)
    input_grad = lax.dot_general(
        proj_grad, out_proj, (((0,), (1,)), ((), ())), preferred_element_type=jnp.float32
    )
    input_grad = input_grad + lax.dot_general(
        pre_grad, out_gate, (((1,), (1,)), ((), ())), preferred_element_type=jnp.float32
    )
    grad_pair = (
        upstream.astype(jnp.float32)
        + norm_back(input_grad.reshape(pair_rep.shape), scaled, inv_std, 2)
    ).astype(jnp.bfloat16)
    grad_proj = lax.dot_general(
        normed, proj_grad, (((0,), (1,)), ((), ())), preferred_element_type=jnp.float32
    )
    grad_gate = lax.dot_general(
        normed, pre_grad, (((0,), (0,)), ((), ())), preferred_element_type=jnp.float32
    )
    grad_final = jnp.dot(tri_normed, out_grad, preferred_element_type=jnp.float32)
    summed = lax.psum((grad_proj, grad_gate, grad_final), ("rows", "chan"))
    two_parts = front(middle, in_proj, in_gate)
    gate_two, left_two, right_two = (two_parts[4], two_parts[5], two_parts[6])
    left_chan, right_chan = (
        lax.all_to_all(left_two, "chan", split_axis=0, concat_axis=2, tiled=True),
        lax.all_to_all(right_two, "chan", split_axis=0, concat_axis=2, tiled=True),
    )
    left_cols = lax.all_to_all(left_chan, "rows", split_axis=2, concat_axis=1, tiled=True)
    tri_two = jnp.einsum(
        "hki,hkj->hij",
        left_cols,
        lax.all_gather(right_chan, "rows", axis=1, tiled=True),
        preferred_element_type=jnp.float32,
    )
    tri_two_pairs = lax.all_to_all(
        tri_two.astype(jnp.bfloat16), "chan", split_axis=2, concat_axis=0, tiled=True
    )
    final_pair = finish(tri_two_pairs, gate_two, in_final, middle, in_drop)[4]
    return (final_pair, grad_pair, summed[0] / N, summed[1] / N, summed[2] / N)


def solution(mesh):
    rows, chan = mesh.shape["rows"], mesh.shape["chan"]
    few = H % (rows * chan) == 0 and chan % rows == 0 and rows & (rows - 1) == 0 and chan & (chan - 1) == 0
    few = few and N // rows >= 128 and N // chan >= 16
    shard = functools.partial(few_shards, rows, chan) if few else shards
    in_specs = (
        P("rows", "chan", None),
        P("rows", "chan", None),
        P(),
        P(),
        P(),
        P(),
        P(),
        P(),
        P("chan", None),
        P("chan", None),
    )
    out_specs = (P("rows", "chan", None), P("rows", "chan", None), P(), P(), P())
    return jax.shard_map(shard, mesh=mesh, in_specs=in_specs, out_specs=out_specs, check_vma=False)
```

```python
import functools

import jax
import jax.numpy as jnp
from jax import lax
from jax.experimental import pallas as pl
from jax.experimental.pallas import tpu as pltpu
from jax.sharding import PartitionSpec as P

N = 512
H = 128

epsilon = 1e-05
keep_rate = 0.75

STEP = 4
GRANT = 40 * 1024 * 1024
F32 = jnp.float32
BF16 = jnp.bfloat16
NN = (((1,), (0,)), ((), ()))
NT = (((1,), (1,)), ((), ()))
TN = (((0,), (0,)), ((), ()))


def mm(a, b, dims=NN):
    return lax.dot_general(a, b, dims, preferred_element_type=F32)


def norm_cols(x):
    average = jnp.mean(x, axis=0, keepdims=True)
    centred = x - average
    inv_std = lax.rsqrt(jnp.mean(centred * centred, axis=0, keepdims=True) + epsilon)
    return centred * inv_std, inv_std


def sides(normed, proj_t, left_ref, right_ref, at):
    hidden = proj_t.shape[0] // 4
    projected = mm(proj_t, normed)
    a_gate, a_val = projected[:hidden], projected[hidden : 2 * hidden]
    b_gate, b_val = projected[2 * hidden : 3 * hidden], projected[3 * hidden :]
    left_ref[at] = (jax.nn.sigmoid(a_gate) * a_val).astype(BF16)
    right_ref[at] = (jax.nn.sigmoid(b_gate) * b_val).astype(BF16)


def front_kernel(pair_ref, proj_ref, left_ref, right_ref):
    for at in range(pair_ref.shape[0]):
        scaled, _ = norm_cols(pair_ref[at].astype(F32))
        sides(scaled.astype(BF16), proj_ref[...], left_ref, right_ref, at)


def middle_kernel(
    tri_ref, pair_ref, up_ref, drop_ref, gate_ref, final_t_ref, final_ref, proj_two_ref,
    mid_ref, tri_grad_ref, pre_ref, left_ref, right_ref, grad_gate_ref, grad_final_ref,
):
    @pl.when(pl.program_id(0) == 0)
    def _():
        grad_gate_ref[...] = jnp.zeros_like(grad_gate_ref)
        grad_final_ref[...] = jnp.zeros_like(grad_final_ref)

    for at in range(tri_ref.shape[0]):
        pair = pair_ref[at].astype(F32)
        normed = norm_cols(pair)[0].astype(BF16)
        gate = jax.nn.sigmoid(mm(gate_ref[...], normed))
        tri_hat, tri_inv = norm_cols(tri_ref[at].astype(F32))
        tri_normed = tri_hat.astype(BF16)
        out_rows = mm(final_t_ref[...], tri_normed)
        drop = drop_ref[at]
        middle = (pair + drop * (gate * out_rows)).astype(BF16)
        mid_ref[at] = middle
        update_grad = up_ref[at].astype(F32) * drop
        out_grad = (update_grad * gate).astype(BF16)
        pre_grad = (update_grad * out_rows * gate * (1.0 - gate)).astype(BF16)
        pre_ref[at] = pre_grad
        normed_grad = mm(final_ref[...], out_grad)
        first = jnp.mean(normed_grad, axis=0, keepdims=True)
        second = jnp.mean(normed_grad * tri_hat, axis=0, keepdims=True)
        tri_grad_ref[at] = (tri_inv * (normed_grad - first - tri_hat * second)).astype(BF16)
        grad_gate_ref[...] += mm(normed, pre_grad, NT)
        grad_final_ref[...] += mm(tri_normed, out_grad, NT)
        normed_two = norm_cols(middle.astype(F32))[0].astype(BF16)
        sides(normed_two, proj_two_ref[...], left_ref, right_ref, at)


def final_kernel(tri_ref, mid_ref, drop_ref, gate_ref, final_t_ref, out_ref):
    for at in range(tri_ref.shape[0]):
        middle = mid_ref[at].astype(F32)
        gate = jax.nn.sigmoid(mm(gate_ref[...], norm_cols(middle)[0].astype(BF16)))
        tri_normed = norm_cols(tri_ref[at].astype(F32))[0].astype(BF16)
        out_rows = mm(final_t_ref[...], tri_normed)
        out_ref[at] = (middle + drop_ref[at] * (gate * out_rows)).astype(BF16)


def pairwise(kernel, by_pair, whole, pair_outs, sum_outs, name):
    steps = by_pair[0].shape[0] // STEP if by_pair[0].shape[0] % STEP == 0 else by_pair[0].shape[0]
    count = by_pair[0].shape[0] // steps
    cut = lambda a: pl.BlockSpec((count,) + a.shape[1:], lambda n: (n, 0, 0))
    full = lambda a: pl.BlockSpec(a.shape, lambda n: (0, 0))
    outs = [jax.ShapeDtypeStruct(by_pair[0].shape, BF16)] * pair_outs
    sums = [jax.ShapeDtypeStruct(s, F32) for s in sum_outs]
    return pl.pallas_call(
        kernel,
        grid=(steps,),
        in_specs=[cut(a) for a in by_pair] + [full(a) for a in whole],
        out_specs=[cut(a) for a in outs] + [full(a) for a in sums],
        out_shape=outs + sums,
        compiler_params=pltpu.CompilerParams(vmem_limit_bytes=GRANT),
        name=name,
    )(*by_pair, *whole)


MESH = pl.DeviceIdType.MESH


def crossed(a, b, size):
    total, bit = 0, 1
    while bit < size:
        total = total + bit * ((a // bit + b // bit) % 2)
        bit *= 2
    return total


def partner(step, rows, chan):
    row = crossed(lax.axis_index("rows"), step // chan, rows)
    col = crossed(lax.axis_index("chan"), step % chan, chan)
    return row, col


def greet(rows, chan):
    barrier = pltpu.get_barrier_semaphore()

    def signal(step, carry):
        pl.semaphore_signal(
            barrier, inc=1, device_id=partner(step, rows, chan), device_id_type=MESH
        )
        return carry

    lax.fori_loop(1, rows * chan, signal, 0)
    pl.semaphore_wait(barrier, rows * chan - 1)


def remote(rows, chan, src, dst, send, recv, at, step):
    row, col = partner(step, rows, chan)
    me = lax.axis_index("rows") * chan + lax.axis_index("chan")
    return pltpu.make_async_remote_copy(
        src.at[row * chan + col],
        dst.at[me],
        send.at[at, step],
        recv.at[at, step],
        device_id=(row, col),
        device_id_type=MESH,
    )


def local(chan, src, dst, send, at):
    me = lax.axis_index("rows") * chan + lax.axis_index("chan")
    return pltpu.make_async_copy(src.at[me], dst.at[me], send.at[at, 0])


def send_all(rows, chan, src, dst, send, recv, at):
    def body(step, carry):
        remote(rows, chan, src, dst, send, recv, at, step).start()
        return carry

    local(chan, src, dst, send, at).start()
    lax.fori_loop(1, rows * chan, body, 0)


def wait_all(rows, chan, src, dst, send, recv, at):
    def body(step, carry):
        remote(rows, chan, src, dst, send, recv, at, step).wait()
        return carry

    local(chan, src, dst, send, at).wait()
    lax.fori_loop(1, rows * chan, body, 0)


def planes(ref, h, rows):
    chan, (_, short, long) = ref.shape[0] // rows, ref.shape[1:]
    return [ref[r * chan : (r + 1) * chan, h].reshape(chan * short, long) for r in range(rows)]


def outgoing_kernel(
    rows, chan, left_in, right_in, left_ref, right_ref, tri_ref, product_ref, send, recv
):
    per, short, long = left_ref.shape[1:]
    part = chan // rows
    moves = [(left_in, left_ref), (right_in, right_ref), (product_ref, tri_ref)]
    greet(rows, chan)
    for at in range(2):
        send_all(rows, chan, *moves[at], send, recv, at)
    for at in range(2):
        wait_all(rows, chan, *moves[at], send, recv, at)

    def body(h, carry):
        left, right = planes(left_ref, h, rows), planes(right_ref, h, rows)
        for r in range(rows):
            for q in range(rows):
                product = mm(right[q], left[r], TN).astype(BF16)
                first = r * chan + q * part
                product_ref[first : first + part, h] = product.reshape(part, short, long)
        return carry

    lax.fori_loop(0, per, body, 0)
    send_all(rows, chan, *moves[2], send, recv, 2)
    wait_all(rows, chan, *moves[2], send, recv, 2)


def backward_kernel(
    rows, chan, grad_in, left_two_in, right_two_in, left_ref, right_ref,
    left_out, right_out, tri_two_ref,
    grad_ref, left_two_ref, right_two_ref, left_grad_ref, right_grad_ref, send, recv,
):
    per, short, long = left_ref.shape[1:]
    moves = [
        (grad_in, grad_ref),
        (left_two_in, left_two_ref),
        (right_two_in, right_two_ref),
        (left_grad_ref, left_out),
        (right_grad_ref, right_out),
    ]
    greet(rows, chan)
    for at in range(3):
        send_all(rows, chan, *moves[at], send, recv, at)
    wait_all(rows, chan, *moves[0], send, recv, 0)

    def back(h, carry):
        grad, left, right = (planes(ref, h, rows) for ref in (grad_ref, left_ref, right_ref))
        for r in range(rows):
            at = slice(r * chan, (r + 1) * chan)
            total = sum(mm(right[q], grad[r][q * long : (q + 1) * long]) for q in range(rows))
            left_grad_ref[at, h] = total.astype(BF16).reshape(chan, short, long)
            total = sum(mm(left[q], grad[q][r * long : (r + 1) * long], NT) for q in range(rows))
            right_grad_ref[at, h] = total.astype(BF16).reshape(chan, short, long)
        return carry

    lax.fori_loop(0, per, back, 0)
    for at in (3, 4):
        send_all(rows, chan, *moves[at], send, recv, at)
    for at in (1, 2):
        wait_all(rows, chan, *moves[at], send, recv, at)

    def two(h, carry):
        left, right = planes(left_two_ref, h, rows), planes(right_two_ref, h, rows)
        for r in range(rows):
            total = sum(mm(right[q], left[q][r * long : (r + 1) * long], NT) for q in range(rows))
            tri_two_ref[r * chan : (r + 1) * chan, h] = total.astype(BF16).reshape(chan, short, long)
        return carry

    lax.fori_loop(0, per, two, 0)
    for at in (3, 4):
        wait_all(rows, chan, *moves[at], send, recv, at)


def fused(kernel, rows, chan, slabs, outs, held, moves, number, name):
    vmem = pl.BlockSpec(memory_space=pltpu.VMEM)
    shape = slabs[0].shape
    return pl.pallas_call(
        functools.partial(kernel, rows, chan),
        in_specs=[vmem] * len(slabs),
        out_specs=[vmem] * outs,
        out_shape=[jax.ShapeDtypeStruct(shape, BF16)] * outs,
        scratch_shapes=[pltpu.VMEM(shape, BF16)] * held
        + [pltpu.SemaphoreType.DMA((moves, rows * chan))] * 2,
        compiler_params=pltpu.CompilerParams(
            collective_id=number, has_side_effects=True, vmem_limit_bytes=GRANT
        ),
        name=name,
    )(*slabs)


def tail_kernel(
    rows, chan,
    tri_in, pair_ref, up_ref, pre_ref, left_ref, right_ref, proj_t_ref, proj_ref, gate_ref, rest_ref,
    tri_ref, grad_ref, sums_ref,
    total_ref, parts_ref, from_chan, held_ref, from_rows, mine_ref, send, recv, small_send, small_recv,
):
    hidden = proj_t_ref.shape[0] // 4
    wide = proj_t_ref.shape[0]
    row, col = lax.axis_index("rows"), lax.axis_index("chan")
    tokens = rows * pair_ref.shape[2]
    greet(rows, chan)
    send_all(rows, chan, tri_in, tri_ref, send, recv, 0)
    total_ref[...] = jnp.zeros_like(total_ref)

    def back(at, carry):
        scaled, inv_std = norm_cols(pair_ref[at].astype(F32))
        normed = scaled.astype(BF16)
        projected = mm(proj_t_ref[...], normed)
        left, right = left_ref[at].astype(F32), right_ref[at].astype(F32)
        left_sig = jax.nn.sigmoid(projected[:hidden])
        right_sig = jax.nn.sigmoid(projected[2 * hidden : 3 * hidden])
        left_val, right_val = left * left_sig, right * right_sig
        proj_grad = jnp.concatenate(
            [
                (left_val * projected[hidden : 2 * hidden] * (1.0 - left_sig)).astype(BF16),
                left_val.astype(BF16),
                (right_val * projected[3 * hidden :] * (1.0 - right_sig)).astype(BF16),
                right_val.astype(BF16),
            ],
            0,
        )
        total_ref[...] += mm(normed, proj_grad, NT)
        input_grad = mm(proj_ref[...], proj_grad) + mm(gate_ref[...], pre_ref[at])
        first = jnp.mean(input_grad, axis=0, keepdims=True)
        second = jnp.mean(input_grad * scaled, axis=0, keepdims=True)
        grad_ref[at] = (
            up_ref[at].astype(F32) + inv_std * (input_grad - first - scaled * second)
        ).astype(BF16)
        return carry

    lax.fori_loop(0, pair_ref.shape[0], back, 0)
    shape = parts_ref.shape[:2]
    parts_ref[:, :, :wide] = total_ref[...].reshape(shape + (wide,))
    parts_ref[:, :, wide:] = rest_ref[...].reshape(shape + (rest_ref.shape[1],))

    def copy(step, src, dst, at):
        to_row, to_col = partner(step, rows, chan)
        return pltpu.make_async_remote_copy(
            src,
            dst,
            small_send.at[at, step],
            small_recv.at[at, step],
            device_id=(to_row, to_col),
            device_id_type=MESH,
        )

    def spread(step):
        return copy(step, parts_ref.at[partner(step, rows, chan)[1]], from_chan.at[col], 0)

    def across(step):
        return copy(step * chan, held_ref, from_rows.at[row], 1)

    def share(step):
        return copy(step, mine_ref, sums_ref.at[col], 2)

    def run(make, count):
        lax.fori_loop(1, count, lambda step, carry: (make(step).start(), carry)[1], 0)
        lax.fori_loop(1, count, lambda step, carry: (make(step).wait(), carry)[1], 0)

    from_chan[col] = parts_ref[col]
    run(spread, chan)
    held_ref[...] = jnp.sum(from_chan[...], axis=0)
    from_rows[row] = held_ref[...]
    run(across, rows)
    mine_ref[...] = jnp.sum(from_rows[...], axis=0) * (1.0 / tokens)
    sums_ref[col] = mine_ref[...]
    run(share, chan)
    wait_all(rows, chan, tri_in, tri_ref, send, recv, 0)


def finish_back(rows, chan, tri_two, by_pair, weights, rest):
    vmem = pl.BlockSpec(memory_space=pltpu.VMEM)
    channels, wide = weights[1].shape
    part, width = channels // chan, wide + rest.shape[1]
    operands = [tri_two, *by_pair, *weights, rest]
    held = [(channels, wide), (chan, part, width), (chan, part, width), (part, width)]
    held += [(rows, part, width), (part, width)]
    count = rows * chan
    return pl.pallas_call(
        functools.partial(tail_kernel, rows, chan),
        in_specs=[vmem] * len(operands),
        out_specs=[vmem] * 3,
        out_shape=[
            jax.ShapeDtypeStruct(tri_two.shape, BF16),
            jax.ShapeDtypeStruct(by_pair[0].shape, BF16),
            jax.ShapeDtypeStruct((chan, part, width), F32),
        ],
        scratch_shapes=[pltpu.VMEM(h, F32) for h in held]
        + [pltpu.SemaphoreType.DMA((1, count))] * 2
        + [pltpu.SemaphoreType.DMA((3, count))] * 2,
        compiler_params=pltpu.CompilerParams(
            collective_id=3, has_side_effects=True, vmem_limit_bytes=GRANT
        ),
        name="finish_back",
    )(*operands)


def few_shards(
    rows, chan,
    pair_rep, upstream, out_proj, out_gate, out_final, in_proj, in_gate, in_final, out_drop, in_drop
):
    long, short, channels = pair_rep.shape
    hidden = out_final.shape[0]
    per = hidden // (rows * chan)

    def to_slab(values):
        return jnp.swapaxes(values, 0, 1).reshape(rows * chan, per, short, long)

    def to_pairs(slab):
        return jnp.swapaxes(slab.reshape(hidden, short, long), 0, 1)

    def column(mask):
        return (mask.astype(F32) / keep_rate)[:, :, None]

    pair = jnp.transpose(pair_rep, (1, 2, 0))
    up = jnp.transpose(upstream, (1, 2, 0))
    out_proj_t, in_proj_t = out_proj.T, in_proj.T
    left, right = pairwise(front_kernel, [pair], [out_proj_t], 2, [], "front")
    left, right, triangle = fused(
        outgoing_kernel, rows, chan, [to_slab(left), to_slab(right)], 3, 1, 3, 1, "outgoing"
    )
    middle, tri_grad, pre_grad, left_two, right_two, grad_gate, grad_final = pairwise(
        middle_kernel,
        [to_pairs(triangle), pair, up, column(out_drop)],
        [out_gate.T, out_final.T, out_final, in_proj_t],
        5,
        [out_gate.shape, out_final.shape],
        "middle",
    )
    slabs = [to_slab(tri_grad), to_slab(left_two), to_slab(right_two), left, right]
    left_grad, right_grad, tri_two = fused(
        backward_kernel, rows, chan, slabs, 3, 5, 5, 2, "backward"
    )
    tri_two, grad_pair, grads = finish_back(
        rows,
        chan,
        tri_two,
        [pair, up, pre_grad, to_pairs(left_grad), to_pairs(right_grad)],
        [out_proj_t, out_proj, out_gate],
        jnp.concatenate([grad_gate, grad_final], 1),
    )
    grads = grads.reshape(channels, -1)
    (final_pair,) = pairwise(
        final_kernel,
        [to_pairs(tri_two), middle, column(in_drop)],
        [in_gate.T, in_final.T],
        1,
        [],
        "final",
    )
    wide = out_proj.shape[1]
    return (
        jnp.transpose(final_pair, (2, 0, 1)),
        jnp.transpose(grad_pair, (2, 0, 1)),
        grads[:, :wide],
        grads[:, wide : wide + channels],
        grads[:, wide + channels :],
    )


def layer_norm(values, along):
    average = jnp.mean(values, axis=along, keepdims=True)
    centred = values - average
    inv_std = lax.rsqrt(jnp.mean(centred * centred, axis=along, keepdims=True) + epsilon)
    return (centred * inv_std, inv_std)


def norm_back(gradient, scaled, inv_std, along):
    first_mean = jnp.mean(gradient, axis=along, keepdims=True)
    second_mean = jnp.mean(gradient * scaled, axis=along, keepdims=True)
    return inv_std * (gradient - first_mean - scaled * second_mean)


def front(pair_in, proj_w, gate_w):
    row_count, col_count, channels = pair_in.shape
    scaled, inv_std = layer_norm(pair_in.astype(jnp.float32), 2)
    normed = scaled.astype(jnp.bfloat16).reshape(-1, channels)
    projected = lax.dot_general(
        proj_w, normed, (((0,), (1,)), ((), ())), preferred_element_type=jnp.float32
    )
    hidden = projected.shape[0] // 4
    gate_act = jax.nn.sigmoid(jnp.dot(normed, gate_w, preferred_element_type=jnp.float32))
    left_proj = (jax.nn.sigmoid(projected[:hidden]) * projected[hidden : 2 * hidden]).astype(
        jnp.bfloat16
    )
    right_proj = (
        jax.nn.sigmoid(projected[2 * hidden : 3 * hidden]) * projected[3 * hidden :]
    ).astype(jnp.bfloat16)
    left_proj = left_proj.reshape(hidden, row_count, col_count)
    right_proj = right_proj.reshape(hidden, row_count, col_count)
    return (scaled, inv_std, normed, projected, gate_act, left_proj, right_proj)


def finish(triangle, gate_act, final_w, pair_in, drop_mask):
    hidden = triangle.shape[0]
    tri_hat, tri_inv = layer_norm(triangle.reshape(hidden, -1).astype(jnp.float32), 0)
    tri_normed = tri_hat.astype(jnp.bfloat16)
    out_rows = lax.dot_general(
        tri_normed, final_w, (((0,), (0,)), ((), ())), preferred_element_type=jnp.float32
    )
    update = gate_act * out_rows
    new_pair = (
        pair_in.astype(jnp.float32)
        + drop_mask.astype(jnp.float32)[None] * update.reshape(pair_in.shape) / keep_rate
    ).astype(jnp.bfloat16)
    return (tri_hat, tri_inv, tri_normed, out_rows, new_pair)


def shards(
    pair_rep, upstream, out_proj, out_gate, out_final, in_proj, in_gate, in_final, out_drop, in_drop
):
    channels = pair_rep.shape[2]
    scaled, inv_std, normed, projected, gate_act, left_proj, right_proj = front(
        pair_rep, out_proj, out_gate
    )
    hidden = left_proj.shape[0]
    left_slab, right_slab = (
        lax.all_to_all(left_proj, "chan", split_axis=0, concat_axis=2, tiled=True),
        lax.all_to_all(right_proj, "chan", split_axis=0, concat_axis=2, tiled=True),
    )
    triangle = jnp.einsum(
        "hik,hjk->hij",
        left_slab,
        lax.all_gather(right_slab, "rows", axis=1, tiled=True),
        preferred_element_type=jnp.float32,
    )
    tri_pairs = lax.all_to_all(
        triangle.astype(jnp.bfloat16), "chan", split_axis=2, concat_axis=0, tiled=True
    )
    tri_hat, tri_inv, tri_normed, out_rows, middle = finish(
        tri_pairs, gate_act, out_final, pair_rep, out_drop
    )
    update_grad = (
        upstream.astype(jnp.float32) * out_drop.astype(jnp.float32)[None] / keep_rate
    ).reshape(-1, channels)
    gate_grad = update_grad * out_rows
    out_grad = (update_grad * gate_act).astype(jnp.bfloat16)
    normed_grad = lax.dot_general(
        out_final, out_grad, (((1,), (1,)), ((), ())), preferred_element_type=jnp.float32
    )
    tri_grad = (
        norm_back(normed_grad, tri_hat, tri_inv, 0).astype(jnp.bfloat16).reshape(left_proj.shape)
    )
    pre_grad = (gate_grad * gate_act * (1.0 - gate_act)).astype(jnp.bfloat16)
    tri_slab = lax.all_to_all(tri_grad, "chan", split_axis=0, concat_axis=2, tiled=True)
    right_again = lax.all_gather(right_slab, "rows", axis=1, tiled=True)
    left_grad = jnp.einsum(
        "hij,hjk->hik", tri_slab, right_again, preferred_element_type=jnp.float32
    ).astype(jnp.bfloat16)
    left_full = lax.all_gather(left_slab, "rows", axis=1, tiled=True)
    tri_cols = lax.all_to_all(tri_slab, "rows", split_axis=2, concat_axis=1, tiled=True)
    right_grad = jnp.einsum(
        "hij,hik->hjk", tri_cols, left_full, preferred_element_type=jnp.float32
    ).astype(jnp.bfloat16)
    left_pairs, right_pairs = (
        lax.all_to_all(left_grad, "chan", split_axis=2, concat_axis=0, tiled=True),
        lax.all_to_all(right_grad, "chan", split_axis=2, concat_axis=0, tiled=True),
    )
    left_back = left_pairs.reshape(hidden, -1).astype(jnp.float32)
    right_back = right_pairs.reshape(hidden, -1).astype(jnp.float32)
    left_sig = jax.nn.sigmoid(projected[:hidden])
    right_sig = jax.nn.sigmoid(projected[2 * hidden : 3 * hidden])
    proj_grad = jnp.concatenate(
        [
            left_back * projected[hidden : 2 * hidden] * left_sig * (1.0 - left_sig),
            left_back * left_sig,
            right_back * projected[3 * hidden :] * right_sig * (1.0 - right_sig),
            right_back * right_sig,
        ],
        0,
    ).astype(jnp.bfloat16)
    input_grad = lax.dot_general(
        proj_grad, out_proj, (((0,), (1,)), ((), ())), preferred_element_type=jnp.float32
    )
    input_grad = input_grad + lax.dot_general(
        pre_grad, out_gate, (((1,), (1,)), ((), ())), preferred_element_type=jnp.float32
    )
    grad_pair = (
        upstream.astype(jnp.float32)
        + norm_back(input_grad.reshape(pair_rep.shape), scaled, inv_std, 2)
    ).astype(jnp.bfloat16)
    grad_proj = lax.dot_general(
        normed, proj_grad, (((0,), (1,)), ((), ())), preferred_element_type=jnp.float32
    )
    grad_gate = lax.dot_general(
        normed, pre_grad, (((0,), (0,)), ((), ())), preferred_element_type=jnp.float32
    )
    grad_final = jnp.dot(tri_normed, out_grad, preferred_element_type=jnp.float32)
    summed = lax.psum((grad_proj, grad_gate, grad_final), ("rows", "chan"))
    two_parts = front(middle, in_proj, in_gate)
    gate_two, left_two, right_two = (two_parts[4], two_parts[5], two_parts[6])
    left_chan, right_chan = (
        lax.all_to_all(left_two, "chan", split_axis=0, concat_axis=2, tiled=True),
        lax.all_to_all(right_two, "chan", split_axis=0, concat_axis=2, tiled=True),
    )
    left_cols = lax.all_to_all(left_chan, "rows", split_axis=2, concat_axis=1, tiled=True)
    tri_two = jnp.einsum(
        "hki,hkj->hij",
        left_cols,
        lax.all_gather(right_chan, "rows", axis=1, tiled=True),
        preferred_element_type=jnp.float32,
    )
    tri_two_pairs = lax.all_to_all(
        tri_two.astype(jnp.bfloat16), "chan", split_axis=2, concat_axis=0, tiled=True
    )
    final_pair = finish(tri_two_pairs, gate_two, in_final, middle, in_drop)[4]
    return (final_pair, grad_pair, summed[0] / N, summed[1] / N, summed[2] / N)


def solution(mesh):
    rows, chan = mesh.shape["rows"], mesh.shape["chan"]
    few = H % (rows * chan) == 0 and chan % rows == 0 and rows & (rows - 1) == 0 and chan & (chan - 1) == 0
    few = few and H % (8 * chan) == 0 and N // rows >= 128 and N // chan >= 16
    shard = functools.partial(few_shards, rows, chan) if few else shards
    in_specs = (
        P("rows", "chan", None),
        P("rows", "chan", None),
        P(),
        P(),
        P(),
        P(),
        P(),
        P(),
        P("chan", None),
        P("chan", None),
    )
    out_specs = (P("rows", "chan", None), P("rows", "chan", None), P(), P(), P())
    return jax.shard_map(shard, mesh=mesh, in_specs=in_specs, out_specs=out_specs, check_vma=False)
```
